32 devices in a mesh: noise: 8 (over z, y), dp: 4 (over x, core).
Axes of the slice: x: 2, y: 2, z: 4, core: 2. Of those that a mesh axis runs over, the one named last changes fastest.
Arguments:
- noise_latents: bfloat16 [2048, 2048], P(('noise', 'dp')), may hold values from -7 to 7
- data_latents: bfloat16 [8192, 2048], P(('dp', 'noise')), may hold values from -16 to 16
Outputs:
- paired_target: bfloat16 [2048, 2048], P('noise', 'dp')
- noise_potential: float32 [2048], P('noise')
- data_potential: float32 [8192], P('dp')
The draws below stay inside these ranges and needn't reach their ends.
All inputs are finite; a program needn't handle non-finite values.
Results may differ from the reference program's by a relative error of at most 0.0046.
Values may be sent and summed in bfloat16 or wider, within the bound.
A program may use at most 64 MiB of HBM per device.

```python
import jax
import jax.numpy as jnp

D = 2048
ITERS = 3
N = 2048
M = 8192


def draw_noise_latents(key, part):
    key = jax.random.fold_in(key, 11)
    values = jnp.clip(jax.random.normal(key, (N, D), jnp.float32), -6.0, 6.0)
    return values.astype(jnp.bfloat16)


def block_levels(own_key, shape, split, low, high):
    level, own = 1.0, jax.random.fold_in(own_key, 6)
    for dim, shards_of in split:
        heights = jnp.exp(jax.random.uniform(jax.random.fold_in(own, dim), (shards_of,), jnp.float32, low / len(split), high / len(split)))
        level = level * jnp.repeat(heights, shape[dim] // shards_of).reshape([-1 if axis == dim else 1 for axis in range(len(shape))])
    return level


def gaussian(stream_key, shape, width, limit, pieces=(), kind=jnp.bfloat16):
    entries = jax.random.normal(stream_key, shape, jnp.float32) * width
    if len(pieces) > 0:
        entries = block_levels(stream_key, shape, pieces, -0.22, 0.18) * entries
    return jnp.clip(entries, min=-limit, max=limit).astype(kind)


def setup_inputs(seed: int = 0) -> dict:
    splits = jax.random.split(jax.random.key(seed), 3)
    return {
        "noise_latents": draw_noise_latents(jax.random.fold_in(splits[2], 71), 0),
        "data_latents": gaussian(splits[1], (M, D), 3.0, 16.0, ((0, 32),)),
    }


smoothing = 0.05


def log_sum(values, axis):
    top = jnp.max(values, axis=axis, keepdims=True)
    return jnp.log(jnp.sum(jnp.exp(values - top), axis=axis)) + jnp.squeeze(top, axis)


def reference(noise_latents, data_latents):
    noise_norms = jnp.sum(jnp.square(noise_latents.astype(jnp.float32)), axis=1)
    data_norms = jnp.sum(jnp.square(data_latents.astype(jnp.float32)), axis=1)
    inner = jnp.dot(noise_latents, data_latents.T, preferred_element_type=jnp.float32)
    cost = (noise_norms[:, None] + data_norms[None, :] - 2.0 * inner) / D
    data_potential = jnp.zeros((M,), jnp.float32)
    noise_potential = jnp.zeros((N,), jnp.float32)
    for step in range(ITERS):
        noise_potential = -smoothing * jnp.log(jnp.float32(N)) - smoothing * log_sum((data_potential[None, :] - cost) / smoothing, 1)
        data_potential = -smoothing * jnp.log(jnp.float32(M)) - smoothing * log_sum((noise_potential[:, None] - cost) / smoothing, 0)
    scores = (data_potential[None, :] - cost) / smoothing
    weights = jax.nn.softmax(scores, axis=1).astype(jnp.bfloat16)
    paired_target = jnp.dot(weights, data_latents, preferred_element_type=jnp.float32).astype(jnp.bfloat16)
    return paired_target, noise_potential, data_potential
```

```python
import functools
import math

import jax
import jax.numpy as jnp
from jax import lax
from jax.experimental import pallas as pl
from jax.experimental.pallas import tpu as pltpu
from jax.sharding import PartitionSpec as P

ITERS = 3


smoothing = 0.05
LOG2E = math.log2(math.e)
MESH = pl.DeviceIdType.MESH
VMEM_LIMIT = 56 * 1024 * 1024


def exp2(a):
    return jnp.exp2(a)


def kernel(
    sizes, noise_ref, data_ref, out_ref, np_ref, dpot_ref,
    nz, dat, scores, w, vcol, lcol, ubuf, lbuf, ybuf, blane, fbuf,
    pk, csend, cbuf, xsend, xbuf, zsend, zbuf,
    dsem, zsem, xsem, csem, lsem, ysem, fsem, rcsem, rxsem, rzsem,
):
    Z, total_rows, total_cols = sizes
    piece, D = noise_ref.shape
    dpiece = data_ref.shape[0]
    rows = 4 * piece
    cols = 2 * dpiece
    width = D // 4
    n = lax.axis_index("noise")
    d = lax.axis_index("dp")
    z, y = n // 2, n % 2
    x, c = d // 2, d % 2
    id_y = (z * 2 + (1 - y), d)
    id_x = (n, (1 - x) * 2 + c)
    id_c = (n, x * 2 + (1 - c))

    def remote(src, dst, sems, index, device):
        return pltpu.make_async_remote_copy(
            src_ref=src, dst_ref=dst, send_sem=sems.at[(0,) + index], recv_sem=sems.at[(1,) + index],
            device_id=device, device_id_type=MESH,
        )

    group = [(zo, do) for zo in range(Z) for do in range(4) if (zo, do) != (0, 0)]

    def member(zo, do):
        return (((z + zo) % Z) * 2 + y, (d + do) % 4)

    barrier = pltpu.get_barrier_semaphore()
    for zo, do in group:
        pl.semaphore_signal(barrier, inc=1, device_id=member(zo, do), device_id_type=MESH)
    pl.semaphore_signal(barrier, inc=1, device_id=id_y, device_id_type=MESH)
    pl.semaphore_wait(barrier, len(group) + 1)

    to_y = remote(data_ref, dat.at[y], dsem, (0,), id_y)
    to_y.start()
    dat[y] = data_ref[...]

    def passed(k, up):
        p = z - k if up else z + k
        return p, (p >= 0 if up else p < Z)

    def along_z(k, up):
        p = z - k if up else z + k
        src = noise_ref if k == 0 else nz.at[p, d]
        return remote(src, nz.at[p, d], zsem, (int(up), k), ((z + 1 if up else z - 1) * 2 + y, d))

    def arrived_z(k, up):
        p = z - k if up else z + k
        return remote(nz.at[p, d], nz.at[p, d], zsem, (int(up), k - 1), ((z - 1 if up else z + 1) * 2 + y, d))

    def over_x(k, up):
        p = z - k if up else z + k
        src = noise_ref if k == 0 else nz.at[p, d]
        return remote(src, nz.at[p, d], xsem, (int(up), k), id_x)

    def arrived_x(k, up):
        p = z - k if up else z + k
        other = (1 - x) * 2 + c
        return remote(nz.at[p, other], nz.at[p, other], xsem, (int(up), k), id_x)

    def over_c(k, up, far):
        p = z - k if up else z + k
        mine = (1 - x) * 2 + c if far else d
        src = noise_ref if (k == 0 and not far) else nz.at[p, mine]
        return remote(src, nz.at[p, mine], csem, (int(far), int(up), k), id_c)

    def arrived_c(k, up, far):
        p = z - k if up else z + k
        theirs = (1 - x) * 2 + (1 - c) if far else x * 2 + (1 - c)
        return remote(nz.at[p, theirs], nz.at[p, theirs], csem, (int(far), int(up), k), id_c)

    def can_go(up):
        return z + 1 < Z if up else z >= 1

    def step_z(k):
        for up in (True, False):
            if k == 0:
                @pl.when(can_go(up))
                def _():
                    along_z(0, up).start()
                if up:
                    over_x(0, True).start()
                    over_c(0, True, False).start()
            else:
                @pl.when(passed(k, up)[1])
                def _():
                    arrived_z(k, up).wait_recv()

                    @pl.when(can_go(up))
                    def _():
                        along_z(k, up).start()
                    over_x(k, up).start()
                    over_c(k, up, False).start()

    def step_x(k):
        for up in (True, False):
            if k == 0 and not up:
                continue

            @pl.when(passed(k, up)[1])
            def _():
                arrived_x(k, up).wait_recv()
                over_c(k, up, True).start()

    step_z(0)
    nz[z, d] = noise_ref[...]
    for k in range(1, Z):
        step_z(k)
        step_x(k - 1)
    step_x(Z - 1)
    for k in range(Z):
        for up in (True, False):
            if k == 0 and not up:
                continue

            @pl.when(passed(k, up)[1])
            def _():
                arrived_c(k, up, False).wait_recv()
                arrived_c(k, up, True).wait_recv()
    remote(dat.at[1 - y], dat.at[1 - y], dsem, (0,), id_y).wait_recv()

    scale = 2.0 * LOG2E / (D * smoothing)
    norm_scale = LOG2E / (D * smoothing)

    def product(b, _):
        block = nz[b].reshape(rows, D)
        scores[:, pl.ds(pl.multiple_of(b * rows, rows), rows)] = scale * lax.dot_general(
            dat[...].reshape(cols, D), block, (((1,), (1,)), ((), ())), preferred_element_type=jnp.float32
        )
        return 0

    lax.fori_loop(0, Z, product, 0)

    def lane_sums(values):
        total = None
        for start in range(0, D, 128):
            part = values[:, start : start + 128].astype(jnp.float32)
            part = part * part
            total = part if total is None else total + part
        return total

    half = lcol
    for yy in range(2):
        half[yy * dpiece : (yy + 1) * dpiece, :] = lane_sums(dat.at[yy])
    blane[...] = jnp.sum(jnp.transpose(half[...]), axis=0, keepdims=True)
    vcol[...] = jnp.broadcast_to(
        -norm_scale * jnp.sum(half[...], axis=1, keepdims=True), (cols, 128)
    )

    def row_lse(r):
        me = z * 4 + d
        for start in range(0, Z * rows, 128):
            t = scores[:, start : start + 128] + vcol[...]
            top = jnp.max(t, axis=0, keepdims=True)
            total = jnp.sum(exp2(t - top), axis=0, keepdims=True)
            lbuf[r, me, :, start : start + 128] = top + jnp.log2(total)
        for zo, do in group:
            remote(lbuf.at[r, me], lbuf.at[r, me], lsem, (r, zo, do), member(zo, do)).start()
        for zo, do in group:
            src = ((z + Z - zo) % Z) * 4 + (d + 4 - do) % 4
            remote(lbuf.at[r, src], lbuf.at[r, src], lsem, (r, zo, do), member(zo, do)).wait_recv()
        parts = [lbuf[r, s] for s in range(4 * Z)]
        top = functools.reduce(jnp.maximum, parts)
        total = functools.reduce(jnp.add, [exp2(a - top) for a in parts])
        return top + jnp.log2(total)

    def pair_lse(a, b):
        top = jnp.maximum(a, b)
        return top + jnp.log2(exp2(a - top) + exp2(b - top))

    def column_lse(r):
        chunk = 64 if cols % 64 == 0 else cols
        for start in range(0, cols, chunk):
            t = scores[start : start + chunk, :] + ubuf[...]
            top = jnp.max(t, axis=1, keepdims=True)
            total = jnp.sum(exp2(t - top), axis=1, keepdims=True)
            lcol[start : start + chunk, :] = jnp.broadcast_to(top, (chunk, 128)) + jnp.log2(
                jnp.broadcast_to(total, (chunk, 128))
            )
        ybuf[r, y] = jnp.transpose(lcol[...])[0:1, :]
        remote(ybuf.at[r, y], ybuf.at[r, y], ysem, (r,), id_y).start()
        remote(ybuf.at[r, 1 - y], ybuf.at[r, 1 - y], ysem, (r,), id_y).wait_recv()
        lane = pair_lse(ybuf[r, 0], ybuf[r, 1])
        vcol[...] = jnp.transpose(jnp.broadcast_to(-math.log2(total_cols) - lane, (128, cols)))
        return lane

    for it in range(ITERS):
        lse = row_lse(it)
        ubuf[...] = -math.log2(total_rows) - lse
        lane = column_lse(it)

    fbuf[z] = -smoothing * math.log(total_cols) - (smoothing / LOG2E) * lane + blane[...] / D
    for zo in range(1, Z):
        remote(fbuf.at[z], fbuf.at[z], fsem, (zo,), member(zo, 0)).start()
    own_norms = jnp.sum(jnp.transpose(lane_sums(nz[z].reshape(rows, D))), axis=0, keepdims=True)
    own_u = ubuf[:, pl.ds(pl.multiple_of(z * rows, rows), rows)]
    np_ref[...] = (
        -smoothing * math.log(total_rows)
        + (smoothing / LOG2E) * (own_u + math.log2(total_rows))
        + own_norms / D
    )

    ubuf[...] = row_lse(ITERS)
    for b in range(Z):
        for start in range(0, rows, 128):
            at = b * rows + start
            t = scores[:, at : at + 128] + vcol[...] - ubuf[:, at : at + 128]
            w[b, start : start + 128, :] = jnp.transpose(exp2(t)).astype(jnp.bfloat16)

    def block(b, column):
        return jnp.dot(
            w[b],
            dat[:, :, pl.ds(pl.multiple_of(column * width, width), width)].reshape(cols, width),
            preferred_element_type=jnp.float32,
        )

    def core_copy(off, far):
        return remote(csend.at[off, far], cbuf.at[off, far], rcsem, (off, far), id_c)

    def x_copy(off):
        return remote(xsend.at[off], xbuf.at[off], rxsem, (off,), id_x)

    def z_copy(off):
        return remote(zsend.at[off - 1], zbuf.at[off - 1], rzsem, (off,), member(off, 0))

    def products(off):
        b = (z + off) % Z
        for far in (1, 0):
            side = 1 - x if far else x
            csend[off, far] = block(b, side * 2 + (1 - c))
            core_copy(off, far).start()
            pk[off, far] = block(b, side * 2 + c)

    def send_x(off):
        core_copy(off, 1).wait_recv()
        xsend[off] = (pk[off, 1] + cbuf[off, 1]).astype(jnp.bfloat16)
        x_copy(off).start()

    order = [Z // 2] + [o for o in range(1, Z) if o != Z // 2] + [0]
    for place, off in enumerate(order):
        products(off)
        if place >= 1:
            send_x(order[place - 1])
    send_x(order[-1])
    for off in order:
        core_copy(off, 0).wait_recv()
        x_copy(off).wait_recv()
        total = pk[off, 0] + cbuf[off, 0] + xbuf[off].astype(jnp.float32)
        if off:
            zsend[off - 1] = total.astype(jnp.bfloat16)
            z_copy(off).start()
        else:
            pk[0, 0] = total
    for zo in range(1, Z):
        src = (z + Z - zo) % Z
        remote(fbuf.at[src], fbuf.at[src], fsem, (zo,), member(zo, 0)).wait_recv()
    dpot_ref[...] = fbuf[...]
    total = pk[0, 0]
    for off in range(1, Z):
        z_copy(off).wait_recv()
        total = total + zbuf[off - 1].astype(jnp.float32)
    out_ref[...] = total.astype(jnp.bfloat16)

    to_y.wait_send()
    for k in range(Z):
        for up in (True, False):
            if k == Z - 1:
                pass
            else:
                @pl.when(jnp.logical_and(passed(k, up)[1], can_go(up)))
                def _():
                    along_z(k, up).wait_send()
            if k == 0 and not up:
                continue

            @pl.when(passed(k, up)[1])
            def _():
                over_x(k, up).wait_send()
                over_c(k, up, False).wait_send()
                over_c(k, up, True).wait_send()
    me = z * 4 + d
    for r in range(ITERS + 1):
        for zo, do in group:
            remote(lbuf.at[r, me], lbuf.at[r, me], lsem, (r, zo, do), member(zo, do)).wait_send()
    for r in range(ITERS):
        remote(ybuf.at[r, y], ybuf.at[r, y], ysem, (r,), id_y).wait_send()
    for zo in range(1, Z):
        remote(fbuf.at[z], fbuf.at[z], fsem, (zo,), member(zo, 0)).wait_send()
    for off in range(Z):
        core_copy(off, 0).wait_send()
        core_copy(off, 1).wait_send()
        x_copy(off).wait_send()
        if off:
            z_copy(off).wait_send()


def scratch(Z, piece, dpiece, D):
    rows, cols, width = 4 * piece, 2 * dpiece, D // 4
    bf16, f32 = jnp.bfloat16, jnp.float32
    arrays = [
        ((Z, 4, piece, D), bf16),
        ((2, dpiece, D), bf16),
        ((cols, Z * rows), f32),
        ((Z, rows, cols), bf16),
        ((cols, 128), f32),
        ((cols, 128), f32),
        ((1, Z * rows), f32),
        ((ITERS + 1, 4 * Z, 1, Z * rows), f32),
        ((ITERS, 2, 1, cols), f32),
        ((1, cols), f32),
        ((Z, 1, cols), f32),
        ((Z, 2, rows, width), f32),
        ((Z, 2, rows, width), f32),
        ((Z, 2, rows, width), f32),
        ((Z, rows, width), bf16),
        ((Z, rows, width), bf16),
        ((Z - 1, rows, width), bf16),
        ((Z - 1, rows, width), bf16),
    ]
    sems = [
        (2, 1), (2, 2, Z), (2, 2, Z), (2, 2, 2, Z), (2, ITERS + 1, Z, 4), (2, ITERS), (2, Z),
        (2, Z, 2), (2, Z), (2, Z),
    ]
    return arrays, sems


def tiled_local(Z, total_rows, total_cols, noise_latents, data_latents):
    piece, D = noise_latents.shape
    dpiece = data_latents.shape[0]
    rows, cols, width = 4 * piece, 2 * dpiece, D // 4
    arrays, sems = scratch(Z, piece, dpiece, D)
    vmem = pl.BlockSpec(memory_space=pltpu.VMEM)
    paired, noise_potential, data_potential = pl.pallas_call(
        functools.partial(kernel, (Z, total_rows, total_cols)),
        out_shape=(
            jax.ShapeDtypeStruct((rows, width), jnp.bfloat16),
            jax.ShapeDtypeStruct((1, rows), jnp.float32),
            jax.ShapeDtypeStruct((Z, 1, cols), jnp.float32),
        ),
        in_specs=[vmem, vmem],
        out_specs=(vmem, vmem, vmem),
        scratch_shapes=[pltpu.VMEM(s, t) for s, t in arrays] + [pltpu.SemaphoreType.DMA(s) for s in sems],
        compiler_params=pltpu.CompilerParams(
            collective_id=0, has_side_effects=True, vmem_limit_bytes=VMEM_LIMIT
        ),
    )(noise_latents, data_latents)
    return paired, noise_potential.reshape(rows), data_potential.reshape(Z * cols)


def gathered_lse(scores, axis, name):
    top = lax.pmax(jnp.max(scores, axis=axis), name)
    total = lax.psum(jnp.sum(jnp.exp(scores - jnp.expand_dims(top, axis)), axis=axis), name)
    return top + jnp.log(total)


def gathered_local(total_rows, total_cols, noise_latents, data_latents):
    rows = lax.all_gather(noise_latents, "dp", axis=0, tiled=True)
    block = lax.all_gather(data_latents, "noise", axis=0, tiled=True)
    row_norms = jnp.sum(jnp.square(rows.astype(jnp.float32)), axis=1)
    col_norms = jnp.sum(jnp.square(block.astype(jnp.float32)), axis=1)
    inner = jnp.dot(rows, block.T, preferred_element_type=jnp.float32)
    cost = (row_norms[:, None] + col_norms[None, :] - 2.0 * inner) / rows.shape[1]
    data_potential = jnp.zeros((cost.shape[1],), jnp.float32)
    for _ in range(ITERS):
        lse = gathered_lse((data_potential[None, :] - cost) / smoothing, 1, "dp")
        noise_potential = -smoothing * math.log(total_rows) - smoothing * lse
        lse = gathered_lse((noise_potential[:, None] - cost) / smoothing, 0, "noise")
        data_potential = -smoothing * math.log(total_cols) - smoothing * lse
    scores = (data_potential[None, :] - cost) / smoothing
    lse = gathered_lse(scores, 1, "dp")
    weights = jnp.exp(scores - lse[:, None]).astype(jnp.bfloat16)
    partial_sum = jnp.dot(weights, block, preferred_element_type=jnp.float32)
    paired_target = lax.psum_scatter(partial_sum, "dp", scatter_dimension=1, tiled=True)
    return paired_target.astype(jnp.bfloat16), noise_potential, data_potential


def solution(mesh):
    noise_size, dp_size = mesh.shape["noise"], mesh.shape["dp"]

    def local(noise_latents, data_latents):
        piece, D = noise_latents.shape
        dpiece = data_latents.shape[0]
        devices = noise_size * dp_size
        totals = (piece * devices, dpiece * devices)
        Z = noise_size // 2
        fits = noise_size % 2 == 0 and dp_size == 4 and Z >= 2
        if fits:
            arrays = scratch(Z, piece, dpiece, D)[0]
            fits = sum(math.prod(s) * jnp.dtype(t).itemsize for s, t in arrays) < VMEM_LIMIT * 3 // 4
        if fits:
            return tiled_local(Z, *totals, noise_latents, data_latents)
        return gathered_local(*totals, noise_latents, data_latents)

    return jax.shard_map(
        local,
        mesh=mesh,
        in_specs=(P(("noise", "dp"), None), P(("dp", "noise"), None)),
        out_specs=(P("noise", "dp"), P("noise"), P("dp")),
        check_vma=False,
    )
```

```python
import functools
import math

import jax
import jax.numpy as jnp
from jax import lax
from jax.experimental import pallas as pl
from jax.experimental.pallas import tpu as pltpu
from jax.sharding import PartitionSpec as P

ITERS = 3


smoothing = 0.05
LOG2E = math.log2(math.e)
MESH = pl.DeviceIdType.MESH
VMEM_LIMIT = 56 * 1024 * 1024


def exp2(a):
    return jnp.exp2(a)


def kernel(
    sizes, noise_ref, data_ref, out_ref, np_ref, dpot_ref,
    nz, dat, scores, w, vcol, lcol, ubuf, lbuf, ybuf, blane, fbuf,
    pk, csend, cbuf, xsend, xbuf, zsend, zbuf,
    sent, dsem, zout, zsem, xsem, csem, lsem, ysem, fsem, rcsem, rxsem, rzsem,
):
    Z, total_rows, total_cols = sizes
    piece, D = noise_ref.shape
    dpiece = data_ref.shape[0]
    rows = 4 * piece
    cols = 2 * dpiece
    width = D // 4
    n = lax.axis_index("noise")
    d = lax.axis_index("dp")
    z, y = n // 2, n % 2
    x, c = d // 2, d % 2
    id_y = (z * 2 + (1 - y), d)
    id_x = (n, (1 - x) * 2 + c)
    id_c = (n, x * 2 + (1 - c))

    def remote(src, dst, send_sem, recv_sem, device):
        return pltpu.make_async_remote_copy(
            src_ref=src, dst_ref=dst, send_sem=send_sem, recv_sem=recv_sem,
            device_id=device, device_id_type=MESH,
        )

    X, C, L, Y, F, RC, RX, RZ, DATA = range(9)

    group = [(zo, do) for zo in range(Z) for do in range(4) if (zo, do) != (0, 0)]

    def member(zo, do):
        return (((z + zo) % Z) * 2 + y, (d + do) % 4)

    barrier = pltpu.get_barrier_semaphore()
    for zo, do in group:
        pl.semaphore_signal(barrier, inc=1, device_id=member(zo, do), device_id_type=MESH)
    pl.semaphore_signal(barrier, inc=1, device_id=id_y, device_id_type=MESH)
    pl.semaphore_wait(barrier, len(group) + 1)

    to_y = remote(data_ref, dat.at[y], sent.at[DATA], dsem.at[0], id_y)
    to_y.start()
    dat[y] = data_ref[...]

    def passed(k, up):
        p = z - k if up else z + k
        return p, (p >= 0 if up else p < Z)

    def along_z(k, up):
        p = z - k if up else z + k
        src = noise_ref if k == 0 else nz.at[p, d]
        return remote(src, nz.at[p, d], zout.at[int(up), k], zsem.at[int(up), k], ((z + 1 if up else z - 1) * 2 + y, d))

    def arrived_z(k, up):
        p = z - k if up else z + k
        return remote(nz.at[p, d], nz.at[p, d], zout.at[int(up), k], zsem.at[int(up), k - 1], ((z - 1 if up else z + 1) * 2 + y, d))

    def over_x(k, up):
        p = z - k if up else z + k
        src = noise_ref if k == 0 else nz.at[p, d]
        return remote(src, nz.at[p, d], sent.at[X], xsem.at[int(up), k], id_x)

    def arrived_x(k, up):
        p = z - k if up else z + k
        other = (1 - x) * 2 + c
        return remote(nz.at[p, other], nz.at[p, other], sent.at[X], xsem.at[int(up), k], id_x)

    def over_c(k, up, far):
        p = z - k if up else z + k
        mine = (1 - x) * 2 + c if far else d
        src = noise_ref if (k == 0 and not far) else nz.at[p, mine]
        return remote(src, nz.at[p, mine], sent.at[C], csem.at[0], id_c)

    def can_go(up):
        return z + 1 < Z if up else z >= 1

    def step_z(k):
        for up in (True, False):
            if k == 0:
                @pl.when(can_go(up))
                def _():
                    along_z(0, up).start()
                if up:
                    over_x(0, True).start()
                    over_c(0, True, False).start()
            else:
                @pl.when(passed(k, up)[1])
                def _():
                    arrived_z(k, up).wait_recv()

                    @pl.when(can_go(up))
                    def _():
                        along_z(k, up).start()
                    over_x(k, up).start()
                    over_c(k, up, False).start()

    def step_x(k):
        for up in (True, False):
            if k == 0 and not up:
                continue

            @pl.when(passed(k, up)[1])
            def _():
                arrived_x(k, up).wait_recv()
                over_c(k, up, True).start()

    step_z(0)
    nz[z, d] = noise_ref[...]
    for k in range(1, Z):
        step_z(k)
        step_x(k - 1)
    step_x(Z - 1)
    def lane_sums(values):
        total = None
        for start in range(0, D, 128):
            part = values[:, start : start + 128].astype(jnp.float32)
            part = part * part
            total = part if total is None else total + part
        return total

    lcol[pl.ds(pl.multiple_of(y * dpiece, dpiece), dpiece), :] = lane_sums(data_ref)

    half_noise = nz.at[:, 0:2]
    remote(half_noise, half_noise, sent.at[C], csem.at[0], id_c).wait_recv()
    remote(dat.at[1 - y], dat.at[1 - y], sent.at[DATA], dsem.at[0], id_y).wait_recv()
    lcol[pl.ds(pl.multiple_of((1 - y) * dpiece, dpiece), dpiece), :] = lane_sums(dat.at[1 - y])

    scale = 2.0 * LOG2E / (D * smoothing)
    norm_scale = LOG2E / (D * smoothing)

    def product(b, _):
        block = nz[b].reshape(rows, D)
        scores[:, pl.ds(pl.multiple_of(b * rows, rows), rows)] = scale * lax.dot_general(
            dat[...].reshape(cols, D), block, (((1,), (1,)), ((), ())), preferred_element_type=jnp.float32
        )
        return 0

    lax.fori_loop(0, Z, product, 0)

    blane[...] = jnp.sum(jnp.transpose(lcol[...]), axis=0, keepdims=True)
    vcol[...] = jnp.broadcast_to(
        -norm_scale * jnp.sum(lcol[...], axis=1, keepdims=True), (cols, 128)
    )

    def row_lse(r):
        me = z * 4 + d
        for start in range(0, Z * rows, 128):
            t = scores[:, start : start + 128] + vcol[...]
            top = jnp.max(t, axis=0, keepdims=True)
            total = jnp.sum(exp2(t - top), axis=0, keepdims=True)
            lbuf[r, me, :, start : start + 128] = top + jnp.log2(total)
        for zo, do in group:
            remote(lbuf.at[r, me], lbuf.at[r, me], sent.at[L], lsem.at[r], member(zo, do)).start()
        others = lbuf.at[r, 0 : 4 * Z - 1]
        remote(others, others, sent.at[L], lsem.at[r], id_c).wait_recv()
        parts = [lbuf[r, s] for s in range(4 * Z)]
        top = functools.reduce(jnp.maximum, parts)
        total = functools.reduce(jnp.add, [exp2(a - top) for a in parts])
        return top + jnp.log2(total)

    def pair_lse(a, b):
        top = jnp.maximum(a, b)
        return top + jnp.log2(exp2(a - top) + exp2(b - top))

    def column_lse(r):
        chunk = 64 if cols % 64 == 0 else cols
        for start in range(0, cols, chunk):
            t = scores[start : start + chunk, :] + ubuf[...]
            top = jnp.max(t, axis=1, keepdims=True)
            total = jnp.sum(exp2(t - top), axis=1, keepdims=True)
            lcol[start : start + chunk, :] = jnp.broadcast_to(top, (chunk, 128)) + jnp.log2(
                jnp.broadcast_to(total, (chunk, 128))
            )
        ybuf[r, y] = jnp.transpose(lcol[...])[0:1, :]
        remote(ybuf.at[r, y], ybuf.at[r, y], sent.at[Y], ysem.at[r], id_y).start()
        remote(ybuf.at[r, 1 - y], ybuf.at[r, 1 - y], sent.at[Y], ysem.at[r], id_y).wait_recv()
        lane = pair_lse(ybuf[r, 0], ybuf[r, 1])
        vcol[...] = jnp.transpose(jnp.broadcast_to(-math.log2(total_cols) - lane, (128, cols)))
        return lane

    for it in range(ITERS):
        lse = row_lse(it)
        ubuf[...] = -math.log2(total_rows) - lse
        lane = column_lse(it)

    fbuf[z] = -smoothing * math.log(total_cols) - (smoothing / LOG2E) * lane + blane[...] / D
    for zo in range(1, Z):
        remote(fbuf.at[z], fbuf.at[z], sent.at[F], fsem.at[0], member(zo, 0)).start()
    own_norms = jnp.sum(jnp.transpose(lane_sums(nz[z].reshape(rows, D))), axis=0, keepdims=True)
    own_u = ubuf[:, pl.ds(pl.multiple_of(z * rows, rows), rows)]
    np_ref[...] = (
        -smoothing * math.log(total_rows)
        + (smoothing / LOG2E) * (own_u + math.log2(total_rows))
        + own_norms / D
    )

    ubuf[...] = row_lse(ITERS)
    for b in range(Z):
        for start in range(0, rows, 128):
            at = b * rows + start
            t = scores[:, at : at + 128] + vcol[...] - ubuf[:, at : at + 128]
            w[b, start : start + 128, :] = jnp.transpose(exp2(t)).astype(jnp.bfloat16)

    part = rows // 2

    def block(b, h, column):
        return jnp.dot(
            w[b, h * part : (h + 1) * part, :],
            dat[:, :, pl.ds(pl.multiple_of(column * width, width), width)].reshape(cols, width),
            preferred_element_type=jnp.float32,
        )

    def core_copy(off, h, far):
        return remote(
            csend.at[off, far, h], cbuf.at[off, far, h], sent.at[RC], rcsem.at[off, far, h], id_c
        )

    def x_copy(off, h):
        return remote(xsend.at[off, h], xbuf.at[off, h], sent.at[RX], rxsem.at[off, h], id_x)

    def z_copy(off, h):
        return remote(zsend.at[off - 1, h], zbuf.at[off - 1, h], sent.at[RZ], rzsem.at[0], member(off, 0))

    def products(off, h):
        b = (z + off) % Z
        for far in (1, 0):
            side = 1 - x if far else x
            csend[off, far, h] = block(b, h, side * 2 + (1 - c))
            core_copy(off, h, far).start()
            pk[off, far, h] = block(b, h, side * 2 + c)

    def send_x(off, h):
        core_copy(off, h, 1).wait_recv()
        xsend[off, h] = (pk[off, 1, h] + cbuf[off, 1, h]).astype(jnp.bfloat16)
        x_copy(off, h).start()

    def finish(off, h):
        core_copy(off, h, 0).wait_recv()
        x_copy(off, h).wait_recv()
        total = pk[off, 0, h] + cbuf[off, 0, h] + xbuf[off, h].astype(jnp.float32)
        if off:
            zsend[off - 1, h] = total.astype(jnp.bfloat16)
            z_copy(off, h).start()
        else:
            pk[0, 0, h] = total

    offsets = [Z // 2] + [o for o in range(1, Z) if o != Z // 2] + [0]
    order = [(off, h) for off in offsets for h in range(2)]
    for place in range(len(order) + 3):
        if place < len(order):
            products(*order[place])
        if 1 <= place <= len(order):
            send_x(*order[place - 1])
        if place >= 3:
            finish(*order[place - 3])
    others = fbuf.at[0 : Z - 1]
    remote(others, others, sent.at[F], fsem.at[0], id_c).wait_recv()
    dpot_ref[...] = fbuf[...]
    remote(zbuf, zbuf, sent.at[RZ], rzsem.at[0], id_c).wait_recv()
    for h in range(2):
        total = pk[0, 0, h]
        for off in range(1, Z):
            total = total + zbuf[off - 1, h].astype(jnp.float32)
        out_ref[h * part : (h + 1) * part, :] = total.astype(jnp.bfloat16)

    to_y.wait_send()
    for k in range(Z - 1):
        for up in (True, False):
            @pl.when(jnp.logical_and(passed(k, up)[1], can_go(up)))
            def _():
                along_z(k, up).wait_send()
    remote(nz.at[:, 0], nz.at[:, 0], sent.at[X], xsem.at[0, 0], id_x).wait_send()
    remote(half_noise, half_noise, sent.at[C], csem.at[0], id_c).wait_send()
    others = lbuf.at[:, 0 : 4 * Z - 1]
    remote(others, others, sent.at[L], lsem.at[0], id_c).wait_send()
    remote(ybuf.at[:, 0], ybuf.at[:, 0], sent.at[Y], ysem.at[0], id_y).wait_send()
    others = fbuf.at[0 : Z - 1]
    remote(others, others, sent.at[F], fsem.at[0], id_c).wait_send()
    remote(csend, cbuf, sent.at[RC], rcsem.at[0, 0, 0], id_c).wait_send()
    remote(xsend, xbuf, sent.at[RX], rxsem.at[0, 0], id_x).wait_send()
    remote(zsend, zbuf, sent.at[RZ], rzsem.at[0], id_c).wait_send()


def scratch(Z, piece, dpiece, D):
    rows, cols, width = 4 * piece, 2 * dpiece, D // 4
    part = rows // 2
    bf16, f32 = jnp.bfloat16, jnp.float32
    arrays = [
        ((Z, 4, piece, D), bf16),
        ((2, dpiece, D), bf16),
        ((cols, Z * rows), f32),
        ((Z, rows, cols), bf16),
        ((cols, 128), f32),
        ((cols, 128), f32),
        ((1, Z * rows), f32),
        ((ITERS + 1, 4 * Z, 1, Z * rows), f32),
        ((ITERS, 2, 1, cols), f32),
        ((1, cols), f32),
        ((Z, 1, cols), f32),
        ((Z, 2, 2, part, width), f32),
        ((Z, 2, 2, part, width), f32),
        ((Z, 2, 2, part, width), f32),
        ((Z, 2, part, width), bf16),
        ((Z, 2, part, width), bf16),
        ((Z - 1, 2, part, width), bf16),
        ((Z - 1, 2, part, width), bf16),
    ]
    sems = [(9,), (1,), (2, Z), (2, Z), (2, Z), (1,), (ITERS + 1,), (ITERS,), (1,), (Z, 2, 2), (Z, 2), (1,)]
    return arrays, sems


def tiled_local(Z, total_rows, total_cols, noise_latents, data_latents):
    piece, D = noise_latents.shape
    dpiece = data_latents.shape[0]
    rows, cols, width = 4 * piece, 2 * dpiece, D // 4
    arrays, sems = scratch(Z, piece, dpiece, D)
    vmem = pl.BlockSpec(memory_space=pltpu.VMEM)
    paired, noise_potential, data_potential = pl.pallas_call(
        functools.partial(kernel, (Z, total_rows, total_cols)),
        out_shape=(
            jax.ShapeDtypeStruct((rows, width), jnp.bfloat16),
            jax.ShapeDtypeStruct((1, rows), jnp.float32),
            jax.ShapeDtypeStruct((Z, 1, cols), jnp.float32),
        ),
        in_specs=[vmem, vmem],
        out_specs=(vmem, vmem, vmem),
        scratch_shapes=[pltpu.VMEM(s, t) for s, t in arrays] + [pltpu.SemaphoreType.DMA(s) for s in sems],
        compiler_params=pltpu.CompilerParams(
            collective_id=0, has_side_effects=True, vmem_limit_bytes=VMEM_LIMIT
        ),
    )(noise_latents, data_latents)
    return paired, noise_potential.reshape(rows), data_potential.reshape(Z * cols)


def gathered_lse(scores, axis, name):
    top = lax.pmax(jnp.max(scores, axis=axis), name)
    total = lax.psum(jnp.sum(jnp.exp(scores - jnp.expand_dims(top, axis)), axis=axis), name)
    return top + jnp.log(total)


def gathered_local(total_rows, total_cols, noise_latents, data_latents):
    rows = lax.all_gather(noise_latents, "dp", axis=0, tiled=True)
    block = lax.all_gather(data_latents, "noise", axis=0, tiled=True)
    row_norms = jnp.sum(jnp.square(rows.astype(jnp.float32)), axis=1)
    col_norms = jnp.sum(jnp.square(block.astype(jnp.float32)), axis=1)
    inner = jnp.dot(rows, block.T, preferred_element_type=jnp.float32)
    cost = (row_norms[:, None] + col_norms[None, :] - 2.0 * inner) / rows.shape[1]
    data_potential = jnp.zeros((cost.shape[1],), jnp.float32)
    for _ in range(ITERS):
        lse = gathered_lse((data_potential[None, :] - cost) / smoothing, 1, "dp")
        noise_potential = -smoothing * math.log(total_rows) - smoothing * lse
        lse = gathered_lse((noise_potential[:, None] - cost) / smoothing, 0, "noise")
        data_potential = -smoothing * math.log(total_cols) - smoothing * lse
    scores = (data_potential[None, :] - cost) / smoothing
    lse = gathered_lse(scores, 1, "dp")
    weights = jnp.exp(scores - lse[:, None]).astype(jnp.bfloat16)
    partial_sum = jnp.dot(weights, block, preferred_element_type=jnp.float32)
    paired_target = lax.psum_scatter(partial_sum, "dp", scatter_dimension=1, tiled=True)
    return paired_target.astype(jnp.bfloat16), noise_potential, data_potential


def solution(mesh):
    noise_size, dp_size = mesh.shape["noise"], mesh.shape["dp"]

    def local(noise_latents, data_latents):
        piece, D = noise_latents.shape
        dpiece = data_latents.shape[0]
        devices = noise_size * dp_size
        totals = (piece * devices, dpiece * devices)
        Z = noise_size // 2
        fits = noise_size % 2 == 0 and dp_size == 4 and Z >= 2
        if fits:
            arrays = scratch(Z, piece, dpiece, D)[0]
            fits = sum(math.prod(s) * jnp.dtype(t).itemsize for s, t in arrays) < VMEM_LIMIT * 3 // 4
        if fits:
            return tiled_local(Z, *totals, noise_latents, data_latents)
        return gathered_local(*totals, noise_latents, data_latents)

    return jax.shard_map(
        local,
        mesh=mesh,
        in_specs=(P(("noise", "dp"), None), P(("dp", "noise"), None)),
        out_specs=(P("noise", "dp"), P("noise"), P("dp")),
        check_vma=False,
    )
```

```python
import functools
import math

import jax
import jax.numpy as jnp
from jax import lax
from jax.experimental import pallas as pl
from jax.experimental.pallas import tpu as pltpu
from jax.sharding import PartitionSpec as P

ITERS = 3


smoothing = 0.05
LOG2E = math.log2(math.e)
MESH = pl.DeviceIdType.MESH
VMEM_LIMIT = 56 * 1024 * 1024


def exp2(a):
    return jnp.exp2(a)


def kernel(
    sizes, noise_ref, data_ref, out_ref, np_ref, dpot_ref,
    nz, dat, scores, w, vcol, lcol, ubuf, lbuf, ybuf, blane, fbuf,
    pk, csend, cbuf, xsend, xbuf, zsend, zbuf, pdat, pscores, pv, pw,
    sent, dsem, zout, zsem, xsem, csem, lsem, ysem, fsem, rcsem, rxsem, rzsem,
    psem, qsem, vsem,
):
    Z, total_rows, total_cols = sizes
    piece, D = noise_ref.shape
    dpiece = data_ref.shape[0]
    rows = 4 * piece
    cols = 2 * dpiece
    width = D // 4
    n = lax.axis_index("noise")
    d = lax.axis_index("dp")
    z, y = n // 2, n % 2
    x, c = d // 2, d % 2
    id_y = (z * 2 + (1 - y), d)
    id_x = (n, (1 - x) * 2 + c)
    id_c = (n, x * 2 + (1 - c))
    id_pair = ((z + 1 - 2 * (z % 2)) * 2 + y, d)

    def remote(src, dst, send_sem, recv_sem, device):
        return pltpu.make_async_remote_copy(
            src_ref=src, dst_ref=dst, send_sem=send_sem, recv_sem=recv_sem,
            device_id=device, device_id_type=MESH,
        )

    X, C, L, Y, F, RC, RX, RZ, DATA, PAIR, PAIR_Y, V = range(12)

    group = [(zo, do) for zo in range(Z) for do in range(4) if (zo, do) != (0, 0)]

    def member(zo, do):
        return (((z + zo) % Z) * 2 + y, (d + do) % 4)

    barrier = pltpu.get_barrier_semaphore()
    for zo, do in group:
        pl.semaphore_signal(barrier, inc=1, device_id=member(zo, do), device_id_type=MESH)
    pl.semaphore_signal(barrier, inc=1, device_id=id_y, device_id_type=MESH)
    pl.semaphore_wait(barrier, len(group) + 1)

    to_y = remote(data_ref, dat.at[y], sent.at[DATA], dsem.at[0], id_y)
    to_y.start()
    dat[y] = data_ref[...]

    def passed(k, up):
        p = z - k if up else z + k
        return p, (p >= 0 if up else p < Z)

    def along_z(k, up):
        p = z - k if up else z + k
        src = noise_ref if k == 0 else nz.at[p, d]
        return remote(src, nz.at[p, d], zout.at[int(up), k], zsem.at[int(up), k], ((z + 1 if up else z - 1) * 2 + y, d))

    def arrived_z(k, up):
        p = z - k if up else z + k
        return remote(nz.at[p, d], nz.at[p, d], zout.at[int(up), k], zsem.at[int(up), k - 1], ((z - 1 if up else z + 1) * 2 + y, d))

    def over_x(k, up):
        p = z - k if up else z + k
        src = noise_ref if k == 0 else nz.at[p, d]
        return remote(src, nz.at[p, d], sent.at[X], xsem.at[int(up), k], id_x)

    def arrived_x(k, up):
        p = z - k if up else z + k
        other = (1 - x) * 2 + c
        return remote(nz.at[p, other], nz.at[p, other], sent.at[X], xsem.at[int(up), k], id_x)

    def over_c(k, up, far):
        p = z - k if up else z + k
        mine = (1 - x) * 2 + c if far else d
        src = noise_ref if (k == 0 and not far) else nz.at[p, mine]
        return remote(src, nz.at[p, mine], sent.at[C], csem.at[0], id_c)

    def can_go(up):
        return z + 1 < Z if up else z >= 1

    def step_z(k):
        for up in (True, False):
            if k == 0:
                @pl.when(can_go(up))
                def _():
                    along_z(0, up).start()
                if up:
                    over_x(0, True).start()
                    over_c(0, True, False).start()
            else:
                @pl.when(passed(k, up)[1])
                def _():
                    arrived_z(k, up).wait_recv()

                    @pl.when(can_go(up))
                    def _():
                        along_z(k, up).start()
                    over_x(k, up).start()
                    over_c(k, up, False).start()

    def step_x(k):
        for up in (True, False):
            if k == 0 and not up:
                continue

            @pl.when(passed(k, up)[1])
            def _():
                arrived_x(k, up).wait_recv()
                over_c(k, up, True).start()

    step_z(0)
    nz[z, d] = noise_ref[...]
    for k in range(1, Z):
        step_z(k)
        step_x(k - 1)
    step_x(Z - 1)
    def lane_sums(values):
        total = None
        for start in range(0, D, 128):
            part = values[:, start : start + 128].astype(jnp.float32)
            part = part * part
            total = part if total is None else total + part
        return total

    lcol[pl.ds(pl.multiple_of(y * dpiece, dpiece), dpiece), :] = lane_sums(data_ref)

    half_noise = nz.at[:, 0:2]
    remote(half_noise, half_noise, sent.at[C], csem.at[0], id_c).wait_recv()
    remote(dat.at[1 - y], dat.at[1 - y], sent.at[DATA], dsem.at[0], id_y).wait_recv()
    lcol[pl.ds(pl.multiple_of((1 - y) * dpiece, dpiece), dpiece), :] = lane_sums(dat.at[1 - y])

    quarter = dpiece // 4

    def pair_copy(q):
        at = pl.ds(q * quarter, quarter)
        return remote(data_ref.at[at], pdat.at[y, at], sent.at[PAIR], psem.at[q], id_pair)

    def pair_copy_y(q):
        at = pl.ds(q * quarter, quarter)
        return remote(pdat.at[y, at], pdat.at[y, at], sent.at[PAIR_Y], qsem.at[0], id_y)

    for q in range(4):
        pair_copy(q).start()

    def forward(q):
        pair_copy(q).wait_recv()
        pair_copy_y(q).start()

    scale = 2.0 * LOG2E / (D * smoothing)
    norm_scale = LOG2E / (D * smoothing)

    def product(b, _):
        block = nz[b].reshape(rows, D)
        scores[:, pl.ds(pl.multiple_of(b * rows, rows), rows)] = scale * lax.dot_general(
            dat[...].reshape(cols, D), block, (((1,), (1,)), ((), ())), preferred_element_type=jnp.float32
        )
        return 0

    lax.fori_loop(0, Z, product, 0)

    blane[...] = jnp.sum(jnp.transpose(lcol[...]), axis=0, keepdims=True)
    vcol[...] = jnp.broadcast_to(
        -norm_scale * jnp.sum(lcol[...], axis=1, keepdims=True), (cols, 128)
    )

    def target(k):
        return (z + 2 * k) % Z

    def pair_product(yy):
        for k in range(Z // 2):
            pscores[k, pl.ds(pl.multiple_of(yy * dpiece, dpiece), dpiece), :] = scale * lax.dot_general(
                pdat[yy], nz[target(k)].reshape(rows, D), (((1,), (1,)), ((), ())),
                preferred_element_type=jnp.float32,
            )

    def row_lse(r, between=lambda: None):
        me = z * 4 + d
        for start in range(0, Z * rows, 128):
            t = scores[:, start : start + 128] + vcol[...]
            top = jnp.max(t, axis=0, keepdims=True)
            total = jnp.sum(exp2(t - top), axis=0, keepdims=True)
            lbuf[r, me, :, start : start + 128] = top + jnp.log2(total)
        for zo, do in group:
            remote(lbuf.at[r, me], lbuf.at[r, me], sent.at[L], lsem.at[r], member(zo, do)).start()
        between()
        others = lbuf.at[r, 0 : 4 * Z - 1]
        remote(others, others, sent.at[L], lsem.at[r], id_c).wait_recv()
        parts = [lbuf[r, s] for s in range(4 * Z)]
        top = functools.reduce(jnp.maximum, parts)
        total = functools.reduce(jnp.add, [exp2(a - top) for a in parts])
        return top + jnp.log2(total)

    def pair_lse(a, b):
        top = jnp.maximum(a, b)
        return top + jnp.log2(exp2(a - top) + exp2(b - top))

    def column_lse(r, between=lambda: None):
        chunk = 64 if cols % 64 == 0 else cols
        for start in range(0, cols, chunk):
            t = scores[start : start + chunk, :] + ubuf[...]
            top = jnp.max(t, axis=1, keepdims=True)
            total = jnp.sum(exp2(t - top), axis=1, keepdims=True)
            lcol[start : start + chunk, :] = jnp.broadcast_to(top, (chunk, 128)) + jnp.log2(
                jnp.broadcast_to(total, (chunk, 128))
            )
        ybuf[r, y] = jnp.transpose(lcol[...])[0:1, :]
        remote(ybuf.at[r, y], ybuf.at[r, y], sent.at[Y], ysem.at[r], id_y).start()
        between()
        remote(ybuf.at[r, 1 - y], ybuf.at[r, 1 - y], sent.at[Y], ysem.at[r], id_y).wait_recv()
        lane = pair_lse(ybuf[r, 0], ybuf[r, 1])
        vcol[...] = jnp.transpose(jnp.broadcast_to(-math.log2(total_cols) - lane, (128, cols)))
        return lane

    for it in range(ITERS):
        lse = row_lse(it, (lambda: forward(2)) if it == 2 else (lambda: None))
        ubuf[...] = -math.log2(total_rows) - lse
        lane = column_lse(it, functools.partial(forward, (0, 1, 3)[it]))

    pv[0] = -math.log2(total_cols) - lane
    remote(pv.at[0], pv.at[1], sent.at[V], vsem.at[0], id_pair).start()
    fbuf[z] = -smoothing * math.log(total_cols) - (smoothing / LOG2E) * lane + blane[...] / D
    for zo in range(1, Z):
        remote(fbuf.at[z], fbuf.at[z], sent.at[F], fsem.at[0], member(zo, 0)).start()
    own_norms = jnp.sum(jnp.transpose(lane_sums(nz[z].reshape(rows, D))), axis=0, keepdims=True)
    own_u = ubuf[:, pl.ds(pl.multiple_of(z * rows, rows), rows)]
    np_ref[...] = (
        -smoothing * math.log(total_rows)
        + (smoothing / LOG2E) * (own_u + math.log2(total_rows))
        + own_norms / D
    )

    ubuf[...] = row_lse(ITERS, lambda: pair_product(y))
    theirs = pdat.at[1 - y]
    remote(theirs, theirs, sent.at[PAIR_Y], qsem.at[0], id_y).wait_recv()
    pair_product(1 - y)
    for k in range(Z // 2):
        for start in range(0, rows, 128):
            at = pl.ds(pl.multiple_of(target(k) * rows + start, 128), 128)
            t = scores[:, at] + vcol[...] - ubuf[:, at]
            w[k, start : start + 128, :] = jnp.transpose(exp2(t)).astype(jnp.bfloat16)
    remote(pv.at[1], pv.at[1], sent.at[V], vsem.at[0], id_pair).wait_recv()
    vcol[...] = jnp.transpose(jnp.broadcast_to(pv[1], (128, cols)))
    for k in range(Z // 2):
        for start in range(0, rows, 128):
            at = pl.ds(pl.multiple_of(target(k) * rows + start, 128), 128)
            t = pscores[k, :, start : start + 128] + vcol[...] - ubuf[:, at]
            pw[k, start : start + 128, :] = jnp.transpose(exp2(t)).astype(jnp.bfloat16)

    part = rows // 2

    def block(k, h, column):
        at = pl.ds(pl.multiple_of(column * width, width), width)
        lines = slice(h * part, (h + 1) * part)
        return jnp.dot(
            w[k, lines, :], dat[:, :, at].reshape(cols, width), preferred_element_type=jnp.float32
        ) + jnp.dot(
            pw[k, lines, :], pdat[:, :, at].reshape(cols, width), preferred_element_type=jnp.float32
        )

    def core_copy(off, h, far):
        return remote(
            csend.at[off, far, h], cbuf.at[off, far, h], sent.at[RC], rcsem.at[off, far, h], id_c
        )

    def x_copy(off, h):
        return remote(xsend.at[off, h], xbuf.at[off, h], sent.at[RX], rxsem.at[off, h], id_x)

    def z_copy(off, h):
        return remote(zsend.at[off - 1, h], zbuf.at[off - 1, h], sent.at[RZ], rzsem.at[0], member(2 * off, 0))

    def products(off, h):
        for far in (1, 0):
            side = 1 - x if far else x
            csend[off, far, h] = block(off, h, side * 2 + (1 - c))
            core_copy(off, h, far).start()
            pk[off, far, h] = block(off, h, side * 2 + c)

    def send_x(off, h):
        core_copy(off, h, 1).wait_recv()
        xsend[off, h] = (pk[off, 1, h] + cbuf[off, 1, h]).astype(jnp.bfloat16)
        x_copy(off, h).start()

    def finish(off, h):
        core_copy(off, h, 0).wait_recv()
        x_copy(off, h).wait_recv()
        total = pk[off, 0, h] + cbuf[off, 0, h] + xbuf[off, h].astype(jnp.float32)
        if off:
            zsend[off - 1, h] = total.astype(jnp.bfloat16)
            z_copy(off, h).start()
        else:
            pk[0, 0, h] = total

    offsets = list(range(1, Z // 2)) + [0]
    order = [(off, h) for off in offsets for h in range(2)]
    for place in range(len(order) + 3):
        if place < len(order):
            products(*order[place])
        if 1 <= place <= len(order):
            send_x(*order[place - 1])
        if place >= 3:
            finish(*order[place - 3])
    others = fbuf.at[0 : Z - 1]
    remote(others, others, sent.at[F], fsem.at[0], id_c).wait_recv()
    dpot_ref[...] = fbuf[...]
    remote(zbuf, zbuf, sent.at[RZ], rzsem.at[0], id_c).wait_recv()
    for h in range(2):
        total = pk[0, 0, h]
        for off in range(1, Z // 2):
            total = total + zbuf[off - 1, h].astype(jnp.float32)
        out_ref[h * part : (h + 1) * part, :] = total.astype(jnp.bfloat16)

    to_y.wait_send()
    for k in range(Z - 1):
        for up in (True, False):
            @pl.when(jnp.logical_and(passed(k, up)[1], can_go(up)))
            def _():
                along_z(k, up).wait_send()
    remote(nz.at[:, 0], nz.at[:, 0], sent.at[X], xsem.at[0, 0], id_x).wait_send()
    remote(half_noise, half_noise, sent.at[C], csem.at[0], id_c).wait_send()
    others = lbuf.at[:, 0 : 4 * Z - 1]
    remote(others, others, sent.at[L], lsem.at[0], id_c).wait_send()
    remote(ybuf.at[:, 0], ybuf.at[:, 0], sent.at[Y], ysem.at[0], id_y).wait_send()
    others = fbuf.at[0 : Z - 1]
    remote(others, others, sent.at[F], fsem.at[0], id_c).wait_send()
    remote(data_ref, pdat.at[y], sent.at[PAIR], psem.at[0], id_pair).wait_send()
    remote(pdat.at[0], pdat.at[0], sent.at[PAIR_Y], qsem.at[0], id_y).wait_send()
    remote(pv.at[0], pv.at[1], sent.at[V], vsem.at[0], id_pair).wait_send()
    remote(csend, cbuf, sent.at[RC], rcsem.at[0, 0, 0], id_c).wait_send()
    remote(xsend, xbuf, sent.at[RX], rxsem.at[0, 0], id_x).wait_send()
    remote(zsend, zbuf, sent.at[RZ], rzsem.at[0], id_c).wait_send()


def scratch(Z, piece, dpiece, D):
    rows, cols, width = 4 * piece, 2 * dpiece, D // 4
    part = rows // 2
    bf16, f32 = jnp.bfloat16, jnp.float32
    arrays = [
        ((Z, 4, piece, D), bf16),
        ((2, dpiece, D), bf16),
        ((cols, Z * rows), f32),
        ((Z // 2, rows, cols), bf16),
        ((cols, 128), f32),
        ((cols, 128), f32),
        ((1, Z * rows), f32),
        ((ITERS + 1, 4 * Z, 1, Z * rows), f32),
        ((ITERS, 2, 1, cols), f32),
        ((1, cols), f32),
        ((Z, 1, cols), f32),
        ((Z // 2, 2, 2, part, width), f32),
        ((Z // 2, 2, 2, part, width), f32),
        ((Z // 2, 2, 2, part, width), f32),
        ((Z // 2, 2, part, width), bf16),
        ((Z // 2, 2, part, width), bf16),
        ((Z // 2 - 1, 2, part, width), bf16),
        ((Z // 2 - 1, 2, part, width), bf16),
        ((2, dpiece, D), bf16),
        ((Z // 2, cols, rows), f32),
        ((2, 1, cols), f32),
        ((Z // 2, rows, cols), bf16),
    ]
    sems = [(12,), (1,), (2, Z), (2, Z), (2, Z), (1,), (ITERS + 1,), (ITERS,), (1,), (Z // 2, 2, 2), (Z // 2, 2), (1,), (4,), (1,), (1,)]
    return arrays, sems


def tiled_local(Z, total_rows, total_cols, noise_latents, data_latents):
    piece, D = noise_latents.shape
    dpiece = data_latents.shape[0]
    rows, cols, width = 4 * piece, 2 * dpiece, D // 4
    arrays, sems = scratch(Z, piece, dpiece, D)
    vmem = pl.BlockSpec(memory_space=pltpu.VMEM)
    paired, noise_potential, data_potential = pl.pallas_call(
        functools.partial(kernel, (Z, total_rows, total_cols)),
        out_shape=(
            jax.ShapeDtypeStruct((rows, width), jnp.bfloat16),
            jax.ShapeDtypeStruct((1, rows), jnp.float32),
            jax.ShapeDtypeStruct((Z, 1, cols), jnp.float32),
        ),
        in_specs=[vmem, vmem],
        out_specs=(vmem, vmem, vmem),
        scratch_shapes=[pltpu.VMEM(s, t) for s, t in arrays] + [pltpu.SemaphoreType.DMA(s) for s in sems],
        compiler_params=pltpu.CompilerParams(
            collective_id=0, has_side_effects=True, vmem_limit_bytes=VMEM_LIMIT
        ),
    )(noise_latents, data_latents)
    return paired, noise_potential.reshape(rows), data_potential.reshape(Z * cols)


def gathered_lse(scores, axis, name):
    top = lax.pmax(jnp.max(scores, axis=axis), name)
    total = lax.psum(jnp.sum(jnp.exp(scores - jnp.expand_dims(top, axis)), axis=axis), name)
    return top + jnp.log(total)


def gathered_local(total_rows, total_cols, noise_latents, data_latents):
    rows = lax.all_gather(noise_latents, "dp", axis=0, tiled=True)
    block = lax.all_gather(data_latents, "noise", axis=0, tiled=True)
    row_norms = jnp.sum(jnp.square(rows.astype(jnp.float32)), axis=1)
    col_norms = jnp.sum(jnp.square(block.astype(jnp.float32)), axis=1)
    inner = jnp.dot(rows, block.T, preferred_element_type=jnp.float32)
    cost = (row_norms[:, None] + col_norms[None, :] - 2.0 * inner) / rows.shape[1]
    data_potential = jnp.zeros((cost.shape[1],), jnp.float32)
    for _ in range(ITERS):
        lse = gathered_lse((data_potential[None, :] - cost) / smoothing, 1, "dp")
        noise_potential = -smoothing * math.log(total_rows) - smoothing * lse
        lse = gathered_lse((noise_potential[:, None] - cost) / smoothing, 0, "noise")
        data_potential = -smoothing * math.log(total_cols) - smoothing * lse
    scores = (data_potential[None, :] - cost) / smoothing
    lse = gathered_lse(scores, 1, "dp")
    weights = jnp.exp(scores - lse[:, None]).astype(jnp.bfloat16)
    partial_sum = jnp.dot(weights, block, preferred_element_type=jnp.float32)
    paired_target = lax.psum_scatter(partial_sum, "dp", scatter_dimension=1, tiled=True)
    return paired_target.astype(jnp.bfloat16), noise_potential, data_potential


def solution(mesh):
    noise_size, dp_size = mesh.shape["noise"], mesh.shape["dp"]

    def local(noise_latents, data_latents):
        piece, D = noise_latents.shape
        dpiece = data_latents.shape[0]
        devices = noise_size * dp_size
        totals = (piece * devices, dpiece * devices)
        Z = noise_size // 2
        fits = noise_size % 2 == 0 and dp_size == 4 and Z >= 4 and Z % 2 == 0 and dpiece % 64 == 0
        if fits:
            arrays = scratch(Z, piece, dpiece, D)[0]
            fits = sum(math.prod(s) * jnp.dtype(t).itemsize for s, t in arrays) < VMEM_LIMIT * 3 // 4
        if fits:
            return tiled_local(Z, *totals, noise_latents, data_latents)
        return gathered_local(*totals, noise_latents, data_latents)

    return jax.shard_map(
        local,
        mesh=mesh,
        in_specs=(P(("noise", "dp"), None), P(("dp", "noise"), None)),
        out_specs=(P("noise", "dp"), P("noise"), P("dp")),
        check_vma=False,
    )
```

```python
import functools
import math

import jax
import jax.numpy as jnp
from jax import lax
from jax.experimental import pallas as pl
from jax.experimental.pallas import tpu as pltpu
from jax.sharding import PartitionSpec as P

ITERS = 3


smoothing = 0.05
LOG2E = math.log2(math.e)
MESH = pl.DeviceIdType.MESH
VMEM_LIMIT = 56 * 1024 * 1024
CHUNKS = 8
FETCH = {
    "start": ((0,), ()),
    "row 0": ((1, 2), (0,)),
    "column 0": ((3,), (1,)),
    "after column 0": ((), (2,)),
    "row 1": ((4, 5), (3,)),
    "column 1": ((6,), (4,)),
    "after column 1": ((), (5,)),
    "row 2": ((7,), (6,)),
    "column 2": ((), (7,)),
}


def exp2(a):
    return jnp.exp2(a)


def kernel(
    sizes, noise_ref, data_ref, out_ref, np_ref, dpot_ref,
    nz, dat, scores, w, vcol, lcol, ubuf, lbuf, ybuf, blane, fbuf,
    pk, csend, cbuf, xsend, xbuf, zsend, zbuf, pdat, pscores, pv, pw,
    sent, dsem, zout, zsem, xsem, csem, lsem, ysem, fsem, rcsem, rxsem, rzsem,
    psem, qsem, vsem,
):
    Z, total_rows, total_cols = sizes
    piece, D = noise_ref.shape
    dpiece = data_ref.shape[0]
    rows = 4 * piece
    cols = 2 * dpiece
    width = D // 4
    n = lax.axis_index("noise")
    d = lax.axis_index("dp")
    z, y = n // 2, n % 2
    x, c = d // 2, d % 2
    id_y = (z * 2 + (1 - y), d)
    id_x = (n, (1 - x) * 2 + c)
    id_c = (n, x * 2 + (1 - c))
    id_pair = ((z + 1 - 2 * (z % 2)) * 2 + y, d)

    def remote(src, dst, send_sem, recv_sem, device):
        return pltpu.make_async_remote_copy(
            src_ref=src, dst_ref=dst, send_sem=send_sem, recv_sem=recv_sem,
            device_id=device, device_id_type=MESH,
        )

    X, C, L, Y, F, RC, RX, RZ, DATA, PAIR, PAIR_Y, V = range(12)

    group = [(zo, do) for zo in range(Z) for do in range(4) if (zo, do) != (0, 0)]

    def member(zo, do):
        return (((z + zo) % Z) * 2 + y, (d + do) % 4)

    barrier = pltpu.get_barrier_semaphore()
    for zo, do in group:
        pl.semaphore_signal(barrier, inc=1, device_id=member(zo, do), device_id_type=MESH)
    pl.semaphore_signal(barrier, inc=1, device_id=id_y, device_id_type=MESH)
    pl.semaphore_wait(barrier, len(group) + 1)

    to_y = remote(data_ref, dat.at[y], sent.at[DATA], dsem.at[0], id_y)
    to_y.start()
    dat[y] = data_ref[...]

    def passed(k, up):
        p = z - k if up else z + k
        return p, (p >= 0 if up else p < Z)

    def along_z(k, up):
        p = z - k if up else z + k
        src = noise_ref if k == 0 else nz.at[p, d]
        return remote(src, nz.at[p, d], zout.at[int(up), k], zsem.at[int(up), k], ((z + 1 if up else z - 1) * 2 + y, d))

    def arrived_z(k, up):
        p = z - k if up else z + k
        return remote(nz.at[p, d], nz.at[p, d], zout.at[int(up), k], zsem.at[int(up), k - 1], ((z - 1 if up else z + 1) * 2 + y, d))

    def over_x(k, up):
        p = z - k if up else z + k
        src = noise_ref if k == 0 else nz.at[p, d]
        return remote(src, nz.at[p, d], sent.at[X], xsem.at[int(up), k], id_x)

    def arrived_x(k, up):
        p = z - k if up else z + k
        other = (1 - x) * 2 + c
        return remote(nz.at[p, other], nz.at[p, other], sent.at[X], xsem.at[int(up), k], id_x)

    def over_c(k, up, far):
        p = z - k if up else z + k
        mine = (1 - x) * 2 + c if far else d
        src = noise_ref if (k == 0 and not far) else nz.at[p, mine]
        return remote(src, nz.at[p, mine], sent.at[C], csem.at[0], id_c)

    def can_go(up):
        return z + 1 < Z if up else z >= 1

    def step_z(k):
        for up in (True, False):
            if k == 0:
                @pl.when(can_go(up))
                def _():
                    along_z(0, up).start()
                if up:
                    over_x(0, True).start()
                    over_c(0, True, False).start()
            else:
                @pl.when(passed(k, up)[1])
                def _():
                    arrived_z(k, up).wait_recv()

                    @pl.when(can_go(up))
                    def _():
                        along_z(k, up).start()
                    over_x(k, up).start()
                    over_c(k, up, False).start()

    def step_x(k):
        for up in (True, False):
            if k == 0 and not up:
                continue

            @pl.when(passed(k, up)[1])
            def _():
                arrived_x(k, up).wait_recv()
                over_c(k, up, True).start()

    step_z(0)
    nz[z, d] = noise_ref[...]
    for k in range(1, Z):
        step_z(k)
        step_x(k - 1)
    step_x(Z - 1)
    def lane_sums(values):
        total = None
        for start in range(0, D, 128):
            part = values[:, start : start + 128].astype(jnp.float32)
            part = part * part
            total = part if total is None else total + part
        return total

    lcol[pl.ds(pl.multiple_of(y * dpiece, dpiece), dpiece), :] = lane_sums(data_ref)

    half_noise = nz.at[:, 0:2]
    remote(half_noise, half_noise, sent.at[C], csem.at[0], id_c).wait_recv()
    remote(dat.at[1 - y], dat.at[1 - y], sent.at[DATA], dsem.at[0], id_y).wait_recv()
    lcol[pl.ds(pl.multiple_of((1 - y) * dpiece, dpiece), dpiece), :] = lane_sums(dat.at[1 - y])

    quarter = dpiece // CHUNKS

    def pair_copy(q):
        at = pl.ds(q * quarter, quarter)
        return remote(data_ref.at[at], pdat.at[y, at], sent.at[PAIR], psem.at[q], id_pair)

    def pair_copy_y(q):
        at = pl.ds(q * quarter, quarter)
        return remote(pdat.at[y, at], pdat.at[y, at], sent.at[PAIR_Y], qsem.at[0], id_y)

    def fetch(point):
        out, onward = FETCH.get(point, ((), ()))
        for q in out:
            pair_copy(q).start()
        for q in onward:
            pair_copy(q).wait_recv()
            pair_copy_y(q).start()

    fetch("start")

    scale = 2.0 * LOG2E / (D * smoothing)
    norm_scale = LOG2E / (D * smoothing)

    def product(b, _):
        block = nz[b].reshape(rows, D)
        scores[:, pl.ds(pl.multiple_of(b * rows, rows), rows)] = scale * lax.dot_general(
            dat[...].reshape(cols, D), block, (((1,), (1,)), ((), ())), preferred_element_type=jnp.float32
        )
        return 0

    lax.fori_loop(0, Z, product, 0)

    blane[...] = jnp.sum(jnp.transpose(lcol[...]), axis=0, keepdims=True)
    vcol[...] = jnp.broadcast_to(
        -norm_scale * jnp.sum(lcol[...], axis=1, keepdims=True), (cols, 128)
    )

    def target(k):
        return (z + 2 * k) % Z

    def pair_product(yy):
        for k in range(Z // 2):
            pscores[k, pl.ds(pl.multiple_of(yy * dpiece, dpiece), dpiece), :] = scale * lax.dot_general(
                pdat[yy], nz[target(k)].reshape(rows, D), (((1,), (1,)), ((), ())),
                preferred_element_type=jnp.float32,
            )

    def row_lse(r, between=lambda: None):
        me = z * 4 + d
        for start in range(0, Z * rows, 128):
            t = scores[:, start : start + 128] + vcol[...]
            top = jnp.max(t, axis=0, keepdims=True)
            total = jnp.sum(exp2(t - top), axis=0, keepdims=True)
            lbuf[r, me, :, start : start + 128] = top + jnp.log2(total)
        for zo, do in group:
            remote(lbuf.at[r, me], lbuf.at[r, me], sent.at[L], lsem.at[r], member(zo, do)).start()
        between()
        others = lbuf.at[r, 0 : 4 * Z - 1]
        remote(others, others, sent.at[L], lsem.at[r], id_c).wait_recv()
        parts = [lbuf[r, s] for s in range(4 * Z)]
        top = functools.reduce(jnp.maximum, parts)
        total = functools.reduce(jnp.add, [exp2(a - top) for a in parts])
        return top + jnp.log2(total)

    def pair_lse(a, b):
        top = jnp.maximum(a, b)
        return top + jnp.log2(exp2(a - top) + exp2(b - top))

    def column_lse(r, between=lambda: None):
        chunk = 64 if cols % 64 == 0 else cols
        for start in range(0, cols, chunk):
            t = scores[start : start + chunk, :] + ubuf[...]
            top = jnp.max(t, axis=1, keepdims=True)
            total = jnp.sum(exp2(t - top), axis=1, keepdims=True)
            lcol[start : start + chunk, :] = jnp.broadcast_to(top, (chunk, 128)) + jnp.log2(
                jnp.broadcast_to(total, (chunk, 128))
            )
        ybuf[r, y] = jnp.transpose(lcol[...])[0:1, :]
        remote(ybuf.at[r, y], ybuf.at[r, y], sent.at[Y], ysem.at[r], id_y).start()
        between()
        remote(ybuf.at[r, 1 - y], ybuf.at[r, 1 - y], sent.at[Y], ysem.at[r], id_y).wait_recv()
        lane = pair_lse(ybuf[r, 0], ybuf[r, 1])
        vcol[...] = jnp.transpose(jnp.broadcast_to(-math.log2(total_cols) - lane, (128, cols)))
        return lane

    for it in range(ITERS):
        lse = row_lse(it, lambda: fetch(f"row {it}"))
        fetch(f"after row {it}")
        ubuf[...] = -math.log2(total_rows) - lse
        lane = column_lse(it, lambda: fetch(f"column {it}"))
        fetch(f"after column {it}")

    pv[0] = -math.log2(total_cols) - lane
    remote(pv.at[0], pv.at[1], sent.at[V], vsem.at[0], id_pair).start()
    fbuf[z] = -smoothing * math.log(total_cols) - (smoothing / LOG2E) * lane + blane[...] / D
    for zo in range(1, Z):
        remote(fbuf.at[z], fbuf.at[z], sent.at[F], fsem.at[0], member(zo, 0)).start()
    own_norms = jnp.sum(jnp.transpose(lane_sums(nz[z].reshape(rows, D))), axis=0, keepdims=True)
    own_u = ubuf[:, pl.ds(pl.multiple_of(z * rows, rows), rows)]
    np_ref[...] = (
        -smoothing * math.log(total_rows)
        + (smoothing / LOG2E) * (own_u + math.log2(total_rows))
        + own_norms / D
    )

    def last():
        fetch(f"row {ITERS}")
        pair_product(y)

    ubuf[...] = row_lse(ITERS, last)
    theirs = pdat.at[1 - y]
    remote(theirs, theirs, sent.at[PAIR_Y], qsem.at[0], id_y).wait_recv()
    pair_product(1 - y)
    for k in range(Z // 2):
        for start in range(0, rows, 128):
            at = pl.ds(pl.multiple_of(target(k) * rows + start, 128), 128)
            t = scores[:, at] + vcol[...] - ubuf[:, at]
            w[k, start : start + 128, :] = jnp.transpose(exp2(t)).astype(jnp.bfloat16)
    remote(pv.at[1], pv.at[1], sent.at[V], vsem.at[0], id_pair).wait_recv()
    vcol[...] = jnp.transpose(jnp.broadcast_to(pv[1], (128, cols)))
    for k in range(Z // 2):
        for start in range(0, rows, 128):
            at = pl.ds(pl.multiple_of(target(k) * rows + start, 128), 128)
            t = pscores[k, :, start : start + 128] + vcol[...] - ubuf[:, at]
            pw[k, start : start + 128, :] = jnp.transpose(exp2(t)).astype(jnp.bfloat16)

    part = rows // 2

    def block(k, h, column):
        at = pl.ds(pl.multiple_of(column * width, width), width)
        lines = slice(h * part, (h + 1) * part)
        return jnp.dot(
            w[k, lines, :], dat[:, :, at].reshape(cols, width), preferred_element_type=jnp.float32
        ) + jnp.dot(
            pw[k, lines, :], pdat[:, :, at].reshape(cols, width), preferred_element_type=jnp.float32
        )

    def core_copy(off, h, far):
        return remote(
            csend.at[off, far, h], cbuf.at[off, far, h], sent.at[RC], rcsem.at[off, far, h], id_c
        )

    def x_copy(off, h):
        return remote(xsend.at[off, h], xbuf.at[off, h], sent.at[RX], rxsem.at[off, h], id_x)

    def z_copy(off, h):
        return remote(zsend.at[off - 1, h], zbuf.at[off - 1, h], sent.at[RZ], rzsem.at[0], member(2 * off, 0))

    def products(off, h):
        for far in (1, 0):
            side = 1 - x if far else x
            csend[off, far, h] = block(off, h, side * 2 + (1 - c))
            core_copy(off, h, far).start()
            pk[off, far, h] = block(off, h, side * 2 + c)

    def send_x(off, h):
        core_copy(off, h, 1).wait_recv()
        xsend[off, h] = (pk[off, 1, h] + cbuf[off, 1, h]).astype(jnp.bfloat16)
        x_copy(off, h).start()

    def finish(off, h):
        core_copy(off, h, 0).wait_recv()
        x_copy(off, h).wait_recv()
        total = pk[off, 0, h] + cbuf[off, 0, h] + xbuf[off, h].astype(jnp.float32)
        if off:
            zsend[off - 1, h] = total.astype(jnp.bfloat16)
            z_copy(off, h).start()
        else:
            pk[0, 0, h] = total

    offsets = list(range(1, Z // 2)) + [0]
    order = [(off, h) for off in offsets for h in range(2)]
    for place in range(len(order) + 3):
        if place < len(order):
            products(*order[place])
        if 1 <= place <= len(order):
            send_x(*order[place - 1])
        if place >= 3:
            finish(*order[place - 3])
    others = fbuf.at[0 : Z - 1]
    remote(others, others, sent.at[F], fsem.at[0], id_c).wait_recv()
    dpot_ref[...] = fbuf[...]
    remote(zbuf, zbuf, sent.at[RZ], rzsem.at[0], id_c).wait_recv()
    for h in range(2):
        total = pk[0, 0, h]
        for off in range(1, Z // 2):
            total = total + zbuf[off - 1, h].astype(jnp.float32)
        out_ref[h * part : (h + 1) * part, :] = total.astype(jnp.bfloat16)

    to_y.wait_send()
    for k in range(Z - 1):
        for up in (True, False):
            @pl.when(jnp.logical_and(passed(k, up)[1], can_go(up)))
            def _():
                along_z(k, up).wait_send()
    remote(nz.at[:, 0], nz.at[:, 0], sent.at[X], xsem.at[0, 0], id_x).wait_send()
    remote(half_noise, half_noise, sent.at[C], csem.at[0], id_c).wait_send()
    others = lbuf.at[:, 0 : 4 * Z - 1]
    remote(others, others, sent.at[L], lsem.at[0], id_c).wait_send()
    remote(ybuf.at[:, 0], ybuf.at[:, 0], sent.at[Y], ysem.at[0], id_y).wait_send()
    others = fbuf.at[0 : Z - 1]
    remote(others, others, sent.at[F], fsem.at[0], id_c).wait_send()
    remote(data_ref, pdat.at[y], sent.at[PAIR], psem.at[0], id_pair).wait_send()
    remote(pdat.at[0], pdat.at[0], sent.at[PAIR_Y], qsem.at[0], id_y).wait_send()
    remote(pv.at[0], pv.at[1], sent.at[V], vsem.at[0], id_pair).wait_send()
    remote(csend, cbuf, sent.at[RC], rcsem.at[0, 0, 0], id_c).wait_send()
    remote(xsend, xbuf, sent.at[RX], rxsem.at[0, 0], id_x).wait_send()
    remote(zsend, zbuf, sent.at[RZ], rzsem.at[0], id_c).wait_send()


def scratch(Z, piece, dpiece, D):
    rows, cols, width = 4 * piece, 2 * dpiece, D // 4
    part = rows // 2
    bf16, f32 = jnp.bfloat16, jnp.float32
    arrays = [
        ((Z, 4, piece, D), bf16),
        ((2, dpiece, D), bf16),
        ((cols, Z * rows), f32),
        ((Z // 2, rows, cols), bf16),
        ((cols, 128), f32),
        ((cols, 128), f32),
        ((1, Z * rows), f32),
        ((ITERS + 1, 4 * Z, 1, Z * rows), f32),
        ((ITERS, 2, 1, cols), f32),
        ((1, cols), f32),
        ((Z, 1, cols), f32),
        ((Z // 2, 2, 2, part, width), f32),
        ((Z // 2, 2, 2, part, width), f32),
        ((Z // 2, 2, 2, part, width), f32),
        ((Z // 2, 2, part, width), bf16),
        ((Z // 2, 2, part, width), bf16),
        ((Z // 2 - 1, 2, part, width), bf16),
        ((Z // 2 - 1, 2, part, width), bf16),
        ((2, dpiece, D), bf16),
        ((Z // 2, cols, rows), f32),
        ((2, 1, cols), f32),
        ((Z // 2, rows, cols), bf16),
    ]
    sems = [(12,), (1,), (2, Z), (2, Z), (2, Z), (1,), (ITERS + 1,), (ITERS,), (1,), (Z // 2, 2, 2), (Z // 2, 2), (1,), (CHUNKS,), (1,), (1,)]
    return arrays, sems


def tiled_local(Z, total_rows, total_cols, noise_latents, data_latents):
    piece, D = noise_latents.shape
    dpiece = data_latents.shape[0]
    rows, cols, width = 4 * piece, 2 * dpiece, D // 4
    arrays, sems = scratch(Z, piece, dpiece, D)
    vmem = pl.BlockSpec(memory_space=pltpu.VMEM)
    paired, noise_potential, data_potential = pl.pallas_call(
        functools.partial(kernel, (Z, total_rows, total_cols)),
        out_shape=(
            jax.ShapeDtypeStruct((rows, width), jnp.bfloat16),
            jax.ShapeDtypeStruct((1, rows), jnp.float32),
            jax.ShapeDtypeStruct((Z, 1, cols), jnp.float32),
        ),
        in_specs=[vmem, vmem],
        out_specs=(vmem, vmem, vmem),
        scratch_shapes=[pltpu.VMEM(s, t) for s, t in arrays] + [pltpu.SemaphoreType.DMA(s) for s in sems],
        compiler_params=pltpu.CompilerParams(
            collective_id=0, has_side_effects=True, vmem_limit_bytes=VMEM_LIMIT
        ),
    )(noise_latents, data_latents)
    return paired, noise_potential.reshape(rows), data_potential.reshape(Z * cols)


def gathered_lse(scores, axis, name):
    top = lax.pmax(jnp.max(scores, axis=axis), name)
    total = lax.psum(jnp.sum(jnp.exp(scores - jnp.expand_dims(top, axis)), axis=axis), name)
    return top + jnp.log(total)


def gathered_local(total_rows, total_cols, noise_latents, data_latents):
    rows = lax.all_gather(noise_latents, "dp", axis=0, tiled=True)
    block = lax.all_gather(data_latents, "noise", axis=0, tiled=True)
    row_norms = jnp.sum(jnp.square(rows.astype(jnp.float32)), axis=1)
    col_norms = jnp.sum(jnp.square(block.astype(jnp.float32)), axis=1)
    inner = jnp.dot(rows, block.T, preferred_element_type=jnp.float32)
    cost = (row_norms[:, None] + col_norms[None, :] - 2.0 * inner) / rows.shape[1]
    data_potential = jnp.zeros((cost.shape[1],), jnp.float32)
    for _ in range(ITERS):
        lse = gathered_lse((data_potential[None, :] - cost) / smoothing, 1, "dp")
        noise_potential = -smoothing * math.log(total_rows) - smoothing * lse
        lse = gathered_lse((noise_potential[:, None] - cost) / smoothing, 0, "noise")
        data_potential = -smoothing * math.log(total_cols) - smoothing * lse
    scores = (data_potential[None, :] - cost) / smoothing
    lse = gathered_lse(scores, 1, "dp")
    weights = jnp.exp(scores - lse[:, None]).astype(jnp.bfloat16)
    partial_sum = jnp.dot(weights, block, preferred_element_type=jnp.float32)
    paired_target = lax.psum_scatter(partial_sum, "dp", scatter_dimension=1, tiled=True)
    return paired_target.astype(jnp.bfloat16), noise_potential, data_potential


def solution(mesh):
    noise_size, dp_size = mesh.shape["noise"], mesh.shape["dp"]

    def local(noise_latents, data_latents):
        piece, D = noise_latents.shape
        dpiece = data_latents.shape[0]
        devices = noise_size * dp_size
        totals = (piece * devices, dpiece * devices)
        Z = noise_size // 2
        fits = noise_size % 2 == 0 and dp_size == 4 and Z >= 4 and Z % 2 == 0 and dpiece % (16 * CHUNKS) == 0
        if fits:
            arrays = scratch(Z, piece, dpiece, D)[0]
            fits = sum(math.prod(s) * jnp.dtype(t).itemsize for s, t in arrays) < VMEM_LIMIT * 3 // 4
        if fits:
            return tiled_local(Z, *totals, noise_latents, data_latents)
        return gathered_local(*totals, noise_latents, data_latents)

    return jax.shard_map(
        local,
        mesh=mesh,
        in_specs=(P(("noise", "dp"), None), P(("dp", "noise"), None)),
        out_specs=(P("noise", "dp"), P("noise"), P("dp")),
        check_vma=False,
    )
```
